32 devices in a mesh: spin: 4 (over y, core), fock: 8 (over z, x).
Axes of the slice: x: 2, y: 2, z: 4, core: 2. Of those that a mesh axis runs over, the one named last changes fastest.
Arguments:
- amplitudes: float32 [2, 8192, 8192], P(None, 'spin', 'fock'), may hold values from -6 to 6
- cutoffs: int32 [8192], P('spin'), may hold values from 256 to 512
- coupling_first: float32 [13], replicated, may hold values from 0.05 to 0.5
- coupling_second: float32 [13], replicated, may hold values from 0.2 to 2
- frozen_coupling: float32 [16], replicated, may hold values from 1 to 4
- frozen_bits: int32 [16], replicated, may hold values from 0 to 1, as said below
- drive_bits: int32 [13], replicated, may hold values 0 or 1
- angles: float32 [13], replicated, may hold values from 0.3 to 1.3
Outputs:
- evolved: float32 [2, 8192, 8192], P(None, 'spin', 'fock')
The draws below stay inside these ranges and needn't reach their ends.
Inputs may be any that keep to these rules, and one draw needn't show every extreme that they name: `cutoffs`: highest level plus one of the first mode that the ladder couples in each spin configuration. `frozen_bits`: between one and four frozen spins have bit 1, the others bit 0.
All inputs are finite; a program needn't handle non-finite values.
Results may differ from the reference program's by a relative error of at most 0.0003.
Values sent between devices are 32-bit elements; how exact they have to be, the bound alone decides.
No kernel may reach another device: no remote copies, remote signals or barrier semaphores. Data moves between devices by JAX's collectives and lax.ppermute only.
A program may use at most 256 MiB of HBM per device.

```python
import math
import jax
import jax.numpy as jnp
from jax import lax

SPINS = 13
FA = 512
FB = 16
FROZEN = 16
DEGREE = 16
CONFIGS = 8192
COLUMNS = 8192


def draw_frozen_bits(key, part):
    keys = jax.random.split(key, 2)
    most_flipped = max(1, FROZEN // 4)
    flipped = jax.random.randint(keys[0], (), 1, most_flipped + 1)
    scores = jax.random.randint(keys[1], (FROZEN,), 0, 1 << 20) * FROZEN + jnp.arange(FROZEN, dtype=jnp.int32)
    ranks = jnp.argsort(jnp.argsort(scores, stable=True), stable=True)
    return (ranks < flipped).astype(jnp.int32)


def with_ends(drawn, own_key, low, high):
    dims = drawn.shape
    spot = [jax.random.randint(jax.random.fold_in(own_key, axis), (), 0, dims[axis]) for axis in range(len(dims))]
    drawn = drawn.at[tuple(spot)].set(low)
    longest = dims.index(max(dims))
    spot[longest] = (spot[longest] + 1) % dims[longest]
    return drawn.at[tuple(spot)].set(high)


def level_of(stream_key, dims, cuts, smallest, top_value):
    factor_of, own = 1.0, jax.random.fold_in(stream_key, 6)
    for position, blocks in cuts:
        heights = jnp.exp(jax.random.uniform(jax.random.fold_in(own, position), (blocks,), jnp.float32, smallest / len(cuts), top_value / len(cuts)))
        factor_of = factor_of * jnp.repeat(heights, dims[position] // blocks).reshape([-1 if axis == position else 1 for axis in range(len(dims))])
    return factor_of


def centred(key, dims, deviation, reach, cuts=(), kind=jnp.bfloat16):
    entries = jax.random.normal(key, dims, jnp.float32) * deviation
    if len(cuts) > 0:
        entries = level_of(key, dims, cuts, -0.22, 0.18) * entries
    return jnp.clip(entries, min=-reach, max=reach).astype(kind)


def setup_inputs(seed: int = 0) -> dict:
    arg_keys = jax.random.split(jax.random.key(seed), 9)
    return {
        "amplitudes": centred(arg_keys[0], (2, CONFIGS, COLUMNS), 1.0, 6.0, ((1, 4), (2, 8)), jnp.float32),
        "cutoffs": with_ends(jax.random.randint(arg_keys[1], (CONFIGS,), FA // 2, FA + 1), jax.random.fold_in(arg_keys[1], 1), FA // 2, FA).astype(jnp.int32),
        "coupling_first": jnp.clip(jnp.exp(jax.random.uniform(arg_keys[2], (SPINS,), jnp.float32, math.log(0.05), math.log(0.5))), 0.05, 0.5),
        "coupling_second": jnp.clip(jnp.exp(jax.random.uniform(arg_keys[3], (SPINS,), jnp.float32, math.log(0.2), math.log(2.0))), 0.2, 2.0),
        "frozen_coupling": jnp.clip(jnp.exp(jax.random.uniform(arg_keys[4], (FROZEN,), jnp.float32, math.log(1.0), math.log(4.0))), 1.0, 4.0),
        "frozen_bits": draw_frozen_bits(jax.random.fold_in(arg_keys[8], 71), 0),
        "drive_bits": with_ends((jax.random.randint(arg_keys[6], (SPINS,), 0, 2) < 1).astype(jnp.int32), jax.random.fold_in(arg_keys[6], 1), 0, 1),
        "angles": jnp.clip(jax.random.uniform(arg_keys[7], (SPINS,), jnp.float32, 0.3, 1.3), 0.3, 1.3),
    }


evolve_time = 12.0
diagonal_first = 0.06
diagonal_second = 0.04
ladder_first = 0.35
ladder_second = 0.1

def bessel_first(term_order, argument):
    running = 0.0
    addend = (argument / 2.0) ** term_order / math.factorial(term_order)
    for serial in range(80):
        running = running + addend
        addend = addend * -(argument * argument / 4.0) / ((serial + 1) * (serial + 1 + term_order))
    return running

def coefficient_table(term_count):
    real_table = []
    imag_table = []
    for term_order in range(term_count + 1):
        magnitude = (1.0 if term_order == 0 else 2.0) * bessel_first(term_order, evolve_time)
        quarter = term_order % 4
        real_table.append(magnitude if quarter == 0 else -magnitude if quarter == 2 else 0.0)
        imag_table.append(-magnitude if quarter == 1 else magnitude if quarter == 3 else 0.0)
    return (real_table, imag_table)

def spin_strengths(config_index, coupling_first, coupling_second, frozen_coupling, frozen_bits):
    spin_bits = config_index[:, None] >> jnp.arange(SPINS, dtype=jnp.int32)[None, :] & 1
    spin_signs = (1 - 2 * spin_bits).astype(jnp.float32)
    frozen_signs = (1 - 2 * frozen_bits).astype(jnp.float32)
    frozen_part = jnp.sum(frozen_coupling * frozen_signs)
    total_first = jnp.sum(coupling_first) + jnp.sum(frozen_coupling)
    strength_first = ladder_first * (lax.optimization_barrier(jnp.sum(spin_signs * coupling_first[None, :], axis=1)) + frozen_part) / total_first
    strength_second = ladder_second * lax.optimization_barrier(jnp.sum(spin_signs * coupling_second[None, :], axis=1)) / jnp.sum(coupling_second)
    return (strength_first, strength_second)

def apply_hamiltonian(padded, first_level, strength_first, strength_second, cutoff_rows):
    column_count = padded.shape[2] - 2 * FB
    center = padded[:, :, FB:FB + column_count]
    lower_level = padded[:, :, :column_count]
    upper_level = padded[:, :, 2 * FB:]
    column = lax.broadcasted_iota(jnp.int32, (1, column_count), 1)
    level_index = first_level + column // FB
    sub_index = column % FB
    cutoff = cutoff_rows[:, None]
    level_float = level_index.astype(jnp.float32)
    sub_float = sub_index.astype(jnp.float32)
    mode_low = jnp.where((level_index >= 1) & (level_index < cutoff), jnp.sqrt(jnp.maximum(level_float, 0.0) / FA), 0.0)
    mode_high = jnp.where((level_index + 1 >= 1) & (level_index + 1 < cutoff), jnp.sqrt(jnp.maximum(level_float + 1.0, 0.0) / FA), 0.0)
    sub_low = jnp.sqrt(sub_float / FB)
    sub_high = jnp.where(sub_index + 1 < FB, jnp.sqrt((sub_float + 1.0) / FB), 0.0)
    diagonal = diagonal_first * (2.0 * level_float / (FA - 1) - 1.0) + diagonal_second * (2.0 * sub_float / (FB - 1) - 1.0)
    previous_sub = jnp.pad(center[:, :, :-1], ((0, 0), (0, 0), (1, 0)))
    next_sub = jnp.pad(center[:, :, 1:], ((0, 0), (0, 0), (0, 1)))
    first_term = strength_first[None, :, None] * (mode_low[None] * lower_level + mode_high[None] * upper_level)
    second_term = strength_second[None, :, None] * (sub_low[None] * previous_sub + sub_high[None] * next_sub)
    return diagonal[None] * center + first_term + second_term

def weighted_term(term_vector, real_weight, imag_weight):
    rotated = jnp.stack([-term_vector[1], term_vector[0]])
    return real_weight * term_vector + imag_weight * rotated

def chebyshev_series(vector, apply_operator, term_count):
    real_table, imag_table = coefficient_table(term_count)
    real_weights = jnp.asarray(real_table, dtype=jnp.float32)
    imag_weights = jnp.asarray(imag_table, dtype=jnp.float32)
    current = apply_operator(vector)
    running = weighted_term(vector, real_weights[0], imag_weights[0]) + weighted_term(current, real_weights[1], imag_weights[1])

    def advance(term_index, loop_state):
        previous, present, total = loop_state
        following = 2.0 * apply_operator(present) - previous
        total = total + weighted_term(following, real_weights[term_index], imag_weights[term_index])
        return (present, following, total)
    loop_state = lax.fori_loop(2, term_count + 1, advance, (vector, current, running))
    return loop_state[2]

def partner_term(own_part, partner, cosine, sine_value, phase_bit, side_sign):
    keep_part = 1.0 - phase_bit
    real_part = cosine * own_part[0] + sine_value * (side_sign * phase_bit * partner[0] + keep_part * partner[1])
    imag_part = cosine * own_part[1] + sine_value * (side_sign * phase_bit * partner[1] - keep_part * partner[0])
    return jnp.stack([real_part, imag_part])

def rotate_bits(vector, bit_list, angles, drive_bits):
    cosines = jnp.cos(angles)
    sine_values = jnp.sin(angles)
    phases = drive_bits.astype(jnp.float32)
    for spin_slot, bit_number in bit_list:
        config_total = vector.shape[1]
        lower_size = 1 << bit_number
        shaped = vector.reshape(2, config_total // (2 * lower_size), 2, lower_size, vector.shape[2])
        lower_half = shaped[:, :, 0]
        upper_half = shaped[:, :, 1]
        new_lower = partner_term(lower_half, upper_half, cosines[spin_slot], sine_values[spin_slot], phases[spin_slot], -1.0)
        new_upper = partner_term(upper_half, lower_half, cosines[spin_slot], sine_values[spin_slot], phases[spin_slot], 1.0)
        vector = jnp.stack([new_lower, new_upper], axis=2).reshape(vector.shape)
    return vector

def reference(amplitudes, cutoffs, coupling_first, coupling_second, frozen_coupling, frozen_bits, drive_bits, angles):
    block_size = min(CONFIGS, 256)
    blocks = CONFIGS // block_size
    config_index = jnp.arange(CONFIGS, dtype=jnp.int32)
    strength_first, strength_second = spin_strengths(config_index, coupling_first, coupling_second, frozen_coupling, frozen_bits)
    stacked = amplitudes.reshape(2, blocks, block_size, COLUMNS).transpose(1, 0, 2, 3)

    def evolve_block(inputs):
        vector, block_first, block_second, block_cutoff = inputs

        def apply_operator(field):
            padded = jnp.pad(field, ((0, 0), (0, 0), (FB, FB)))
            return apply_hamiltonian(padded, 0, block_first, block_second, block_cutoff)
        return chebyshev_series(vector, apply_operator, DEGREE)
    evolved_blocks = lax.map(evolve_block, (stacked, strength_first.reshape(blocks, block_size), strength_second.reshape(blocks, block_size), cutoffs.reshape(blocks, block_size)))
    propagated = evolved_blocks.transpose(1, 0, 2, 3).reshape(2, CONFIGS, COLUMNS)
    return rotate_bits(propagated, [(slot, slot) for slot in range(SPINS)], angles, drive_bits)
```

```python
import functools
import math

import jax
import jax.numpy as jnp
from jax import lax
from jax.experimental import pallas as pl
from jax.experimental.pallas import tpu as pltpu
from jax.sharding import PartitionSpec as P

SPINS = 13
FA = 512
FB = 16
DEGREE = 16

evolve_time = 12.0
diagonal_first = 0.06
diagonal_second = 0.04
ladder_first = 0.35
ladder_second = 0.1

LANES = 128
ROWS = 8
HALF = ROWS // 2
CUTS = 2
PARTS = 2 * CUTS
GROUP = 128
LOW_BITS = 7
VMEM_LIMIT = 48 * 1024 * 1024
NO_COST = pl.CostEstimate(flops=1, bytes_accessed=1, transcendentals=0)


def bessel_first(term_order, argument):
    running = 0.0
    addend = (argument / 2.0) ** term_order / math.factorial(term_order)
    for serial in range(80):
        running = running + addend
        addend = addend * -(argument * argument / 4.0) / ((serial + 1) * (serial + 1 + term_order))
    return running


def series_weights(term_count):
    weights = []
    for order in range(term_count + 1):
        magnitude = (1.0 if order == 0 else 2.0) * bessel_first(order, evolve_time)
        weights.append(magnitude if order % 4 in (0, 3) else -magnitude)
    return weights


def low_matrix(cosines, sines):
    out = lax.broadcasted_iota(jnp.int32, (GROUP, GROUP), 0)
    into = lax.broadcasted_iota(jnp.int32, (GROUP, GROUP), 1)
    result = jnp.ones((GROUP, GROUP), jnp.float32)
    for spin in range(LOW_BITS):
        out_bit, in_bit = (out >> spin) & 1, (into >> spin) & 1
        crossing = jnp.where(out_bit == 1, sines[spin], -sines[spin])
        result = result * jnp.where(out_bit == in_bit, cosines[spin], crossing)
    return result


def phase_of(config, drive_ref):
    quarter = jnp.zeros(config.shape, jnp.int32)
    for spin in range(SPINS):
        quarter = quarter + ((config >> spin) & 1) * (1 - drive_ref[spin])
    quarter = quarter & 3
    real = jnp.where(quarter == 0, 1.0, jnp.where(quarter == 2, -1.0, 0.0))
    imag = jnp.where(quarter == 1, 1.0, jnp.where(quarter == 3, -1.0, 0.0))
    return real, imag


def scalar_sum(ref):
    total = ref[0]
    for index in range(1, ref.shape[0]):
        total = total + ref[index]
    return total


SCALARS = pl.BlockSpec(memory_space=pltpu.SMEM)


def tied(value, *earlier):
    return lax.optimization_barrier((value, *earlier))[0]


def prepare_kernel(drive_ref, cosines, sines, matrix_ref, phases_ref):
    count = phases_ref.shape[0]
    matrix_ref[...] = low_matrix(cosines, sines)
    first_config = lax.axis_index("spin") * count
    column = lax.broadcasted_iota(jnp.int32, (GROUP, 8), 1)

    def fill(group, carry):
        config = first_config + group * GROUP + lax.broadcasted_iota(jnp.int32, (GROUP, 8), 0)
        real, imag = phase_of(config, drive_ref)
        rows = pl.ds(pl.multiple_of(group * GROUP, GROUP), GROUP)
        phases_ref[rows, :] = jnp.where(column == 0, real, imag)
        return carry

    lax.fori_loop(0, count // GROUP, fill, 0)


def prepare(drive_bits, cosines, sines, count):
    return pl.pallas_call(
        prepare_kernel,
        in_specs=[SCALARS] * 3,
        out_shape=[
            jax.ShapeDtypeStruct((GROUP, GROUP), jnp.float32),
            jax.ShapeDtypeStruct((count, 8), jnp.float32),
        ],
        cost_estimate=NO_COST,
        name="prepare",
    )(drive_bits, cosines, sines)


def series_kernel(
    weights,
    halves,
    flip,
    first_unit,
    first_coupling_ref,
    second_coupling_ref,
    frozen_coupling_ref,
    frozen_bits_ref,
    drive_ref,
    cutoff_ref,
    left_ref,
    middle_ref,
    right_ref,
    *refs,
):
    out_refs = refs[:PARTS]
    source, swapped, even_buffer, odd_buffer, ladder, diagonal = refs[PARTS:]
    halo_tiles = left_ref.shape[3] // LANES
    own_tiles = middle_ref.shape[3] // LANES
    tiles = halo_tiles + own_tiles + halo_tiles
    levels_per_tile = LANES // FB
    levels = tiles * levels_per_tile
    mirrored = halves == 2
    segments = HALF // halves
    depth = levels // segments
    block = FB * ROWS
    row = lax.broadcasted_iota(jnp.int32, (ROWS, LANES), 0)
    side = jnp.where(row < HALF, -1.0, 1.0)
    segment_row = row % segments
    first_level = lax.axis_index("fock") * (own_tiles * levels_per_tile) - DEGREE

    def level_at(index):
        if mirrored:
            return first_level + jnp.where(segment_row == 0, index, levels - 1 - index)
        return first_level + segment_row * depth + index

    def link_at(index):
        if mirrored:
            return first_level + jnp.where(segment_row == 0, index, levels - index)
        return level_at(index)

    def place_of(level):
        segment, index = divmod(level, depth)
        return segment, depth - 1 - index if mirrored and segment == 1 else index

    def register(index, sub):
        return pl.ds(pl.multiple_of(index * block + sub * ROWS, ROWS), ROWS)

    @pl.when(pl.program_id(0) == 0)
    def _():
        def fill(index, carry):
            level = level_at(index).astype(jnp.float32)
            first = diagonal_first * (2.0 * level / (FA - 1) - 1.0)
            for sub in range(FB):
                second = diagonal_second * (2.0 * sub / (FB - 1) - 1.0)
                diagonal[register(index, sub), :] = 2.0 * (first + second)
            return carry

        lax.fori_loop(0, depth, fill, 0)

    units_here = (1 << SPINS) // (GROUP * halves) // lax.axis_size("spin")
    unit = (lax.axis_index("spin") ^ flip) * units_here + first_unit + pl.program_id(0)
    half_row = (row % HALF) // segments
    lane = lax.broadcasted_iota(jnp.int32, (ROWS, LANES), 1)
    config = (unit * halves + half_row) * GROUP + lane
    sum_first = jnp.zeros((ROWS, LANES), jnp.float32)
    sum_second = jnp.zeros((ROWS, LANES), jnp.float32)
    for spin in range(SPINS):
        sign = (1 - 2 * ((config >> spin) & 1)).astype(jnp.float32)
        sum_first = sum_first + sign * first_coupling_ref[spin]
        sum_second = sum_second + sign * second_coupling_ref[spin]
    frozen_part = 0.0
    for index in range(frozen_bits_ref.shape[0]):
        frozen_sign = (1 - 2 * frozen_bits_ref[index]).astype(jnp.float32)
        frozen_part = frozen_part + frozen_coupling_ref[index] * frozen_sign
    total_first = scalar_sum(first_coupling_ref) + scalar_sum(frozen_coupling_ref)
    total_second = scalar_sum(second_coupling_ref)
    first = (2.0 * ladder_first) * (sum_first + frozen_part) / total_first
    second = (2.0 * ladder_second) * sum_second / total_second
    cutoff = jnp.broadcast_to(cutoff_ref[:, :LANES], (ROWS, LANES))
    if halves == 2:
        upper_cutoff = jnp.broadcast_to(cutoff_ref[:, LANES:], (ROWS, LANES))
        cutoff = jnp.where(half_row == 0, cutoff, upper_cutoff)
    cutoff = cutoff.astype(jnp.float32)
    phase_real, phase_imag = phase_of(config, drive_ref)
    for index in range(depth + 1):
        level_index = link_at(index)
        level = level_index.astype(jnp.float32)
        root = jnp.sqrt(jnp.maximum(level, 0.0) / FA)
        ladder[index * ROWS : (index + 1) * ROWS, :] = jnp.where(
            (level_index >= 1) & (level < cutoff), root * first, 0.0
        )
    sub_ladder = [second * math.sqrt(sub / FB) for sub in range(FB)]

    def start_of(component, half, level):
        segment, index = place_of(level)
        return (index + 1) * block + component * HALF + half * segments + segment

    for component in range(2):
        for half in range(halves):
            for tile in range(tiles):
                if tile < halo_tiles:
                    taken, place = left_ref, tile
                elif tile < halo_tiles + own_tiles:
                    taken, place = middle_ref, tile - halo_tiles
                else:
                    taken, place = right_ref, tile - halo_tiles - own_tiles
                turned = taken[component, half, :, place * LANES : (place + 1) * LANES].T
                for inner in range(levels_per_tile):
                    start = start_of(component, half, tile * levels_per_tile + inner)
                    source[pl.ds(start, FB, stride=ROWS), :] = turned[
                        inner * FB : (inner + 1) * FB
                    ]

    def fill_ghosts(buffer):
        for sub in range(FB):
            last = buffer[register(depth, sub), :]
            if mirrored:
                other = jnp.where(
                    segment_row == 0, pltpu.roll(last, ROWS - 1, 0), pltpu.roll(last, 1, 0)
                )
                buffer[register(depth + 1, sub), :] = other
            else:
                buffer[register(0, sub), :] = pltpu.roll(last, 1, 0)
                buffer[register(depth + 1, sub), :] = pltpu.roll(
                    buffer[register(1, sub), :], ROWS - 1, 0
                )

    if mirrored:
        for buffer in (even_buffer, odd_buffer):
            buffer[:block, :] = jnp.zeros((block, LANES), jnp.float32)

    terms = len(weights) - 1

    def begin(index, carry):
        for sub in range(FB):
            here = register(index, sub)
            value = source[here, :]
            swapped[here, :] = side * pltpu.roll(value, HALF, 0)
            even_buffer[here, :] = weights[terms] * value
        return carry

    lax.fori_loop(1, depth + 1, begin, 0)
    fill_ghosts(even_buffer)

    for order in range(terms - 1, -1, -1):
        target, present = (odd_buffer, even_buffer) if order % 2 else (even_buffer, odd_buffer)
        given = swapped if order % 2 else source

        def level_step(index, carry):
            lower = ladder[pl.ds(pl.multiple_of((index - 1) * ROWS, ROWS), ROWS), :]
            upper = ladder[pl.ds(pl.multiple_of(index * ROWS, ROWS), ROWS), :]
            centre = [present[register(index, sub), :] for sub in range(FB)]
            for sub in range(FB):
                here = register(index, sub)
                total = diagonal[register(index - 1, sub), :] * centre[sub]
                total += lower * present[register(index - 1, sub), :]
                total += upper * present[register(index + 1, sub), :]
                if sub > 0:
                    total += sub_ladder[sub] * centre[sub - 1]
                if sub + 1 < FB:
                    total += sub_ladder[sub + 1] * centre[sub + 1]
                if order == 0:
                    total = 0.5 * total
                addend = weights[order] * given[here, :]
                if order < terms - 1:
                    addend -= target[here, :]
                total += addend
                if order == 0:
                    turned = pltpu.roll(total, HALF, 0)
                    total = phase_real * total + phase_imag * (side * turned)
                target[here, :] = total
            return carry

        skipped = (terms - order) // 4 * 4 if mirrored else 0
        lax.fori_loop(1 + skipped, depth + 1, level_step, 0, unroll=4)
        if order > 0:
            fill_ghosts(target)

    for component in range(2):
        for half in range(halves):
            for level in range(own_tiles * levels_per_tile):
                start = start_of(component, half, level + halo_tiles * levels_per_tile)
                out_ref = out_refs[component * CUTS + level * FB // out_refs[0].shape[1]]
                first_row = level * FB % out_ref.shape[1]
                out_ref[half, first_row : first_row + FB, :] = even_buffer[
                    pl.ds(start, FB, stride=ROWS), :
                ]


def series_piece(scalars, cutoffs, sides, side_start, middle, first_group, groups, flip):
    width = middle.shape[3]
    left, right = sides
    halo = left.shape[3]
    halves = 2 if all(number % 2 == 0 for number in (first_group, groups, side_start)) else 1
    segments = HALF // halves
    depth = (width + 2 * halo) // FB // segments
    field = pltpu.VMEM(((depth + 2) * FB * ROWS, LANES), jnp.float32)
    first_unit, first_side = first_group // halves, side_start // halves
    return pl.pallas_call(
        functools.partial(series_kernel, series_weights(DEGREE), halves, flip, first_unit),
        grid=(groups // halves,),
        in_specs=[SCALARS] * len(scalars)
        + [
            pl.BlockSpec((1, GROUP * halves), lambda i: (0, i + first_unit)),
            pl.BlockSpec((2, halves, GROUP, halo), lambda i: (0, i + first_side, 0, 0)),
            pl.BlockSpec((2, halves, GROUP, width), lambda i: (0, i + first_unit, 0, 0)),
            pl.BlockSpec((2, halves, GROUP, halo), lambda i: (0, i + first_side, 0, 0)),
        ],
        out_specs=[pl.BlockSpec((halves, width // CUTS, GROUP), lambda i: (i, 0, 0))] * PARTS,
        out_shape=[jax.ShapeDtypeStruct((groups, width // CUTS, GROUP), jnp.float32)] * PARTS,
        scratch_shapes=[
            field,
            field,
            field,
            field,
            pltpu.VMEM(((depth + 1) * ROWS, LANES), jnp.float32),
            pltpu.VMEM((depth * FB * ROWS, LANES), jnp.float32),
        ],
        compiler_params=pltpu.CompilerParams(vmem_limit_bytes=VMEM_LIMIT),
        cost_estimate=NO_COST,
        name="series",
    )(*scalars, cutoffs, left, middle, right)


def mix_kernel(spin, cosines, sines, matrix_ref, *refs):
    own_refs, other_refs, out_refs = refs[:PARTS], refs[PARTS : 2 * PARTS], refs[2 * PARTS :]
    side = (2 * (lax.axis_index("spin") & 1) - 1).astype(jnp.float32)
    cosine = cosines[spin]
    sine = side * sines[spin]
    matrix = matrix_ref[...]
    length = own_refs[0].shape[1]
    for part in range(PARTS):
        component, cut = divmod(part, CUTS)
        mixed = lax.dot_general(
            matrix,
            cosine * own_refs[part][0] + sine * other_refs[part][0],
            (((1,), (1,)), ((), ())),
            precision=lax.Precision.HIGHEST,
            preferred_element_type=jnp.float32,
        )
        start = 0
        for out_ref in out_refs:
            stop = start + out_ref.shape[3]
            low, high = max(start, cut * length), min(stop, (cut + 1) * length)
            if low < high:
                out_ref[component, 0, :, low - start : high - start] = mixed[
                    :, low - cut * length : high - cut * length
                ]
            start = stop


def mix_piece(spin, cosines, sines, matrix, own, other, widths):
    groups, length = own[0].shape[:2]
    spec = pl.BlockSpec((1, length, GROUP), lambda i: (i, 0, 0))
    return pl.pallas_call(
        functools.partial(mix_kernel, spin),
        grid=(groups,),
        in_specs=[SCALARS, SCALARS, pl.BlockSpec((GROUP, GROUP), lambda i: (0, 0))]
        + [spec] * (2 * PARTS),
        out_specs=[pl.BlockSpec((2, 1, GROUP, width), lambda i: (0, i, 0, 0)) for width in widths],
        out_shape=[jax.ShapeDtypeStruct((2, groups, GROUP, width), jnp.float32) for width in widths],
        compiler_params=pltpu.CompilerParams(vmem_limit_bytes=VMEM_LIMIT),
        cost_estimate=NO_COST,
        name="mix",
    )(cosines, sines, matrix, *own, *other)


def join_kernel(counts, far_spin, cosines, sines, phase_ref, *refs):
    pieces = len(counts)
    own_refs, other_refs, out_ref = refs[:pieces], refs[pieces : 2 * pieces], refs[-1]
    groups = sum(counts)
    bits = groups.bit_length() - 1
    width = out_ref.shape[3]
    far_sine = (lax.axis_index("spin") & 2).astype(jnp.float32) * sines[far_spin] - sines[far_spin]
    places = [(piece, index) for piece in range(pieces) for index in range(counts[piece])]

    def row_tile(step, carry):
        rows = pl.ds(pl.multiple_of(step * ROWS, ROWS), ROWS)
        for lanes in range(width // LANES):
            columns = slice(lanes * LANES, (lanes + 1) * LANES)
            fields = []
            for component in range(2):
                field = [
                    cosines[far_spin] * own_refs[piece][component, index, rows, columns]
                    + far_sine * other_refs[piece][component, index, rows, columns]
                    for piece, index in places
                ]
                for bit in range(bits):
                    cosine, sine = cosines[LOW_BITS + bit], sines[LOW_BITS + bit]
                    following = list(field)
                    for group in range(groups):
                        if not (group >> bit) & 1:
                            partner = group | (1 << bit)
                            lower, upper = field[group], field[partner]
                            following[group] = cosine * lower - sine * upper
                            following[partner] = cosine * upper + sine * lower
                    field = following
                fields.append(field)
            for group in range(groups):
                entry = phase_ref[group, rows, :]
                phase_real = jnp.broadcast_to(entry[:, 0:1], (ROWS, LANES))
                phase_imag = jnp.broadcast_to(entry[:, 1:2], (ROWS, LANES))
                real, imag = fields[0][group], fields[1][group]
                out_ref[0, group, rows, columns] = phase_real * real + phase_imag * imag
                out_ref[1, group, rows, columns] = phase_real * imag - phase_imag * real
        return carry

    lax.fori_loop(0, out_ref.shape[2] // ROWS, row_tile, 0)


def join_chunk(far_spin, cosines, sines, table, own, other, target, start, width, out_shape):
    counts = [piece.shape[1] for piece in own]
    groups = sum(counts)
    depth = GROUP // 2
    chunk = start // width

    def spec(piece):
        place = chunk if piece.shape[3] > width else 0
        return pl.BlockSpec((2, piece.shape[1], depth, width), lambda i: (0, 0, i, place))

    operands = [cosines, sines, table, *own, *other]
    in_specs = [
        SCALARS,
        SCALARS,
        pl.BlockSpec((groups, depth, 8), lambda i: (0, i, 0)),
        *[spec(piece) for piece in [*own, *other]],
    ]
    aliases = {}
    if target is not None:
        aliases = {len(operands): 0}
        operands.append(target)
        in_specs.append(pl.BlockSpec(memory_space=pl.ANY))
    return pl.pallas_call(
        functools.partial(join_kernel, counts, far_spin),
        grid=(GROUP // depth,),
        in_specs=in_specs,
        out_specs=pl.BlockSpec((2, groups, depth, width), lambda i: (0, 0, i, chunk)),
        out_shape=jax.ShapeDtypeStruct(out_shape, jnp.float32),
        input_output_aliases=aliases,
        compiler_params=pltpu.CompilerParams(vmem_limit_bytes=VMEM_LIMIT),
        cost_estimate=NO_COST,
        name="join",
    )(*operands)


def partner_term(own_part, partner, cosine, sine_value, phase_bit, side_sign):
    keep_part = 1.0 - phase_bit
    real_part = cosine * own_part[0] + sine_value * (
        side_sign * phase_bit * partner[0] + keep_part * partner[1]
    )
    imag_part = cosine * own_part[1] + sine_value * (
        side_sign * phase_bit * partner[1] - keep_part * partner[0]
    )
    return jnp.stack([real_part, imag_part])


def piece_sizes(groups):
    if groups >= 16:
        unit = groups // 16
        sizes = [2 * unit, unit, unit, 2 * unit, 2 * unit, 2 * unit, 2 * unit]
    else:
        sizes = [2, 1, 1]
    return [*sizes, groups - sum(sizes)]


def halo_batches(count):
    batches = [1] * min(count, 4)
    while sum(batches) < count:
        batches.append(min(2, count - sum(batches)))
    return batches


def chunk_widths(width):
    wide = 2 * LANES
    return [wide] * (width // wide - 1) + [LANES, LANES]


def per_device(
    amplitudes,
    cutoffs,
    coupling_first,
    coupling_second,
    frozen_coupling,
    frozen_bits,
    drive_bits,
    angles,
):
    local_configs, width = amplitudes.shape[1:]
    groups = local_configs // GROUP
    local_bits = local_configs.bit_length() - 1
    halo = DEGREE * FB
    spin_count = lax.axis_size("spin")
    fock_count = lax.axis_size("fock")
    spin_place = lax.axis_index("spin")
    core_moves = [(i, i ^ 1) for i in range(spin_count)]
    far_moves = [(i, i ^ 2) for i in range(spin_count)]
    up = [(i, i + 1) for i in range(fock_count - 1)]
    down = [(j, i) for i, j in up]
    core_spin, far_spin = local_bits, local_bits + 1

    field = amplitudes.reshape(2, groups, GROUP, width)
    sizes = piece_sizes(groups)
    starts = [sum(sizes[:index]) for index in range(len(sizes))]
    raw_groups = sizes[0]
    raw = lax.ppermute(field[:, :raw_groups], "spin", far_moves)
    raw_cutoffs = lax.ppermute(cutoffs[: raw_groups * GROUP], "spin", far_moves).reshape(1, -1)
    cutoffs = cutoffs.reshape(1, -1)
    cosines, sines = jnp.cos(angles), jnp.sin(angles)
    matrix, phases = prepare(drive_bits, cosines, sines, local_configs)
    phases = phases.reshape(groups, GROUP, 8)
    others = (coupling_second, frozen_coupling, frozen_bits, drive_bits)

    pieces = [(field, cutoffs, start, size, 0) for start, size in zip(starts, sizes)]
    work = [*pieces[1:], (raw, raw_cutoffs, 0, raw_groups, 2), pieces[0]]
    last = len(pieces) - 2
    batches = halo_batches(last)
    batches += [1, 2]
    halos = []
    sent = []
    evolved = []
    crossed = []
    own, other = [], []

    def send_halo(*earlier):
        batch = work[len(halos) : len(halos) + batches[len(sent)]]
        edges = []
        for low, high in ((width - halo, width), (0, halo)):
            cuts = [source[:, start : start + size, :, low:high] for source, _, start, size, _ in batch]
            edges.append(jnp.concatenate(cuts, axis=1) if len(cuts) > 1 else cuts[0])
        if earlier:
            edges = lax.optimization_barrier((*edges, *earlier))[:2]
        sent.append((lax.ppermute(edges[0], "fock", up), lax.ppermute(edges[1], "fock", down)))
        place = 0
        for piece in batch:
            halos.append((sent[-1], place))
            place += piece[3]

    def series(*earlier):
        index = len(evolved)
        source, cuts, start, size, flip = work[index]
        scalars = (tied(coupling_first, *earlier), *others)
        piece = series_piece(scalars, cuts, *halos[index], source, start, size, flip)
        evolved.append(piece)
        crossed.append([lax.ppermute(part, "spin", core_moves) for part in piece])
        return piece[0]

    def mix(index, *earlier):
        widths = chunk_widths(width) if index == last else [width]
        cosine = tied(cosines, *earlier)
        mixed = mix_piece(
            core_spin, cosine, sines, matrix, evolved[index], crossed[index], widths
        )
        if index < last:
            own.append(mixed[0])
            other.append(lax.ppermute(mixed[0], "spin", far_moves))
        return mixed

    latest = matrix
    send_halo()
    prompt = min(4, last)
    for index in range(len(work)):
        waits = [latest]
        if index == 2:
            waits.append(raw)
        elif 2 < index < 6 and len(other) > index - 3:
            waits.append(other[index - 3])
        elif index > last and len(other) > index - 4:
            waits.append(other[index - 4])
        if len(sent) < len(batches):
            send_halo(*halos[index][0])
        latest = series(*waits)
        if index < prompt:
            latest = mix(index, latest)[0]
        elif prompt < index <= last + 1:
            last_pieces = mix(index - 1, latest)
            latest = last_pieces[0]
    (raw_other,) = mix(last + 1, latest)
    (raw_own,) = mix(last + 2, raw_other, other[-1])
    own, other = [raw_own, *own], [raw_other, *other]
    received = []
    result = None
    start = 0
    for chunk, piece in enumerate(last_pieces):
        going = piece if chunk < 2 else tied(piece, received[chunk - 2], raw_own)
        received.append(lax.ppermute(going, "spin", far_moves))
    for chunk, piece in enumerate(last_pieces):
        result = join_chunk(
            far_spin,
            cosines,
            sines,
            phases,
            [*own, piece],
            [*other, received[chunk]],
            result,
            start,
            piece.shape[3],
            field.shape,
        )
        start += piece.shape[3]
    result = result.reshape(amplitudes.shape)
    for bit in range(2, spin_count.bit_length() - 1):
        spin = local_bits + bit
        partner = lax.ppermute(result, "spin", [(i, i ^ (1 << bit)) for i in range(spin_count)])
        side = jnp.where((spin_place >> bit) & 1 == 1, 1.0, -1.0)
        result = partner_term(
            result, partner, cosines[spin], sines[spin], drive_bits[spin].astype(jnp.float32), side
        )
    return result


def solution(mesh):
    placed = (P(None, "spin", "fock"), P("spin"), P(), P(), P(), P(), P(), P())
    return jax.shard_map(
        per_device, mesh=mesh, in_specs=placed, out_specs=P(None, "spin", "fock"), check_vma=False
    )
```

```python
import functools
import math

import jax
import jax.numpy as jnp
from jax import lax
from jax.experimental import pallas as pl
from jax.experimental.pallas import tpu as pltpu
from jax.sharding import PartitionSpec as P

SPINS = 13
FA = 512
FB = 16
DEGREE = 16

evolve_time = 12.0
diagonal_first = 0.06
diagonal_second = 0.04
ladder_first = 0.35
ladder_second = 0.1

LANES = 128
ROWS = 8
HALF = ROWS // 2
GROUP = 128
LOW_BITS = 7
VMEM_LIMIT = 48 * 1024 * 1024
SERIES_FLOPS, SERIES_BYTES = 100_000_000, 300_000
NO_COST = pl.CostEstimate(flops=1, bytes_accessed=1, transcendentals=0)


def bessel_first(term_order, argument):
    running = 0.0
    addend = (argument / 2.0) ** term_order / math.factorial(term_order)
    for serial in range(80):
        running = running + addend
        addend = addend * -(argument * argument / 4.0) / ((serial + 1) * (serial + 1 + term_order))
    return running


def series_weights(term_count):
    weights = []
    for order in range(term_count + 1):
        magnitude = (1.0 if order == 0 else 2.0) * bessel_first(order, evolve_time)
        weights.append(magnitude if order % 4 in (0, 3) else -magnitude)
    return weights


def low_matrix(cosines, sines):
    out = lax.broadcasted_iota(jnp.int32, (GROUP, GROUP), 0)
    into = lax.broadcasted_iota(jnp.int32, (GROUP, GROUP), 1)
    result = jnp.ones((GROUP, GROUP), jnp.float32)
    for spin in range(LOW_BITS):
        out_bit, in_bit = (out >> spin) & 1, (into >> spin) & 1
        crossing = jnp.where(out_bit == 1, sines[spin], -sines[spin])
        result = result * jnp.where(out_bit == in_bit, cosines[spin], crossing)
    return result


def phase_of(config, drive_ref):
    quarter = jnp.zeros(config.shape, jnp.int32)
    for spin in range(SPINS):
        quarter = quarter + ((config >> spin) & 1) * (1 - drive_ref[spin])
    quarter = quarter & 3
    real = jnp.where(quarter == 0, 1.0, jnp.where(quarter == 2, -1.0, 0.0))
    imag = jnp.where(quarter == 1, 1.0, jnp.where(quarter == 3, -1.0, 0.0))
    return real, imag


def scalar_sum(ref):
    total = ref[0]
    for index in range(1, ref.shape[0]):
        total = total + ref[index]
    return total


SCALARS = pl.BlockSpec(memory_space=pltpu.SMEM)


def tied(value, *earlier):
    return lax.optimization_barrier((value, *earlier))[0]


def prepare_kernel(drive_ref, cosines, sines, matrix_ref, phases_ref):
    count = phases_ref.shape[0]
    matrix_ref[...] = low_matrix(cosines, sines)
    first_config = lax.axis_index("spin") * count
    column = lax.broadcasted_iota(jnp.int32, (GROUP, 8), 1)

    def fill(group, carry):
        config = first_config + group * GROUP + lax.broadcasted_iota(jnp.int32, (GROUP, 8), 0)
        real, imag = phase_of(config, drive_ref)
        rows = pl.ds(pl.multiple_of(group * GROUP, GROUP), GROUP)
        phases_ref[rows, :] = jnp.where(column == 0, real, imag)
        return carry

    lax.fori_loop(0, count // GROUP, fill, 0)


def prepare(drive_bits, cosines, sines, count):
    return pl.pallas_call(
        prepare_kernel,
        in_specs=[SCALARS] * 3,
        out_shape=[
            jax.ShapeDtypeStruct((GROUP, GROUP), jnp.float32),
            jax.ShapeDtypeStruct((count, 8), jnp.float32),
        ],
        cost_estimate=pl.CostEstimate(
            flops=8_000_000_000, bytes_accessed=24_000_000, transcendentals=0
        ),
        name="prepare",
    )(drive_bits, cosines, sines)


def series_kernel(
    weights,
    halves,
    flip,
    first_unit,
    first_coupling_ref,
    second_coupling_ref,
    frozen_coupling_ref,
    frozen_bits_ref,
    drive_ref,
    matrix_ref,
    cutoff_ref,
    left_ref,
    middle_ref,
    right_ref,
    *refs,
):
    out_refs = refs[:-6]
    source, swapped, even_buffer, odd_buffer, ladder, diagonal = refs[-6:]
    halo_tiles = left_ref.shape[3] // LANES
    own_tiles = middle_ref.shape[3] // LANES
    tiles = halo_tiles + own_tiles + halo_tiles
    levels_per_tile = LANES // FB
    levels = tiles * levels_per_tile
    mirrored = halves == 2
    segments = HALF // halves
    depth = levels // segments
    block = FB * ROWS
    row = lax.broadcasted_iota(jnp.int32, (ROWS, LANES), 0)
    side = jnp.where(row < HALF, -1.0, 1.0)
    segment_row = row % segments
    first_level = lax.axis_index("fock") * (own_tiles * levels_per_tile) - DEGREE

    def level_at(index):
        if mirrored:
            return first_level + jnp.where(segment_row == 0, index, levels - 1 - index)
        return first_level + segment_row * depth + index

    def link_at(index):
        if mirrored:
            return first_level + jnp.where(segment_row == 0, index, levels - index)
        return level_at(index)

    def place_of(level):
        segment, index = divmod(level, depth)
        return segment, depth - 1 - index if mirrored and segment == 1 else index

    def register(index, sub):
        return pl.ds(pl.multiple_of(index * block + sub * ROWS, ROWS), ROWS)

    @pl.when(pl.program_id(0) == 0)
    def _():
        def fill(index, carry):
            level = level_at(index).astype(jnp.float32)
            first = diagonal_first * (2.0 * level / (FA - 1) - 1.0)
            for sub in range(FB):
                second = diagonal_second * (2.0 * sub / (FB - 1) - 1.0)
                diagonal[register(index, sub), :] = 2.0 * (first + second)
            return carry

        lax.fori_loop(0, depth, fill, 0)

    units_here = (1 << SPINS) // (GROUP * halves) // lax.axis_size("spin")
    unit = (lax.axis_index("spin") ^ flip) * units_here + first_unit + pl.program_id(0)
    half_row = (row % HALF) // segments
    lane = lax.broadcasted_iota(jnp.int32, (ROWS, LANES), 1)
    config = (unit * halves + half_row) * GROUP + lane
    sum_first = jnp.zeros((ROWS, LANES), jnp.float32)
    sum_second = jnp.zeros((ROWS, LANES), jnp.float32)
    for spin in range(SPINS):
        sign = (1 - 2 * ((config >> spin) & 1)).astype(jnp.float32)
        sum_first = sum_first + sign * first_coupling_ref[spin]
        sum_second = sum_second + sign * second_coupling_ref[spin]
    frozen_part = 0.0
    for index in range(frozen_bits_ref.shape[0]):
        frozen_sign = (1 - 2 * frozen_bits_ref[index]).astype(jnp.float32)
        frozen_part = frozen_part + frozen_coupling_ref[index] * frozen_sign
    total_first = scalar_sum(first_coupling_ref) + scalar_sum(frozen_coupling_ref)
    total_second = scalar_sum(second_coupling_ref)
    first = (2.0 * ladder_first) * (sum_first + frozen_part) / total_first
    second = (2.0 * ladder_second) * sum_second / total_second
    cutoff = jnp.broadcast_to(cutoff_ref[:, :LANES], (ROWS, LANES))
    if halves == 2:
        upper_cutoff = jnp.broadcast_to(cutoff_ref[:, LANES:], (ROWS, LANES))
        cutoff = jnp.where(half_row == 0, cutoff, upper_cutoff)
    cutoff = cutoff.astype(jnp.float32)
    phase_real, phase_imag = phase_of(config, drive_ref)
    for index in range(depth + 1):
        level_index = link_at(index)
        level = level_index.astype(jnp.float32)
        root = jnp.sqrt(jnp.maximum(level, 0.0) / FA)
        ladder[index * ROWS : (index + 1) * ROWS, :] = jnp.where(
            (level_index >= 1) & (level < cutoff), root * first, 0.0
        )
    sub_ladder = [second * math.sqrt(sub / FB) for sub in range(FB)]

    def start_of(component, half, level):
        segment, index = place_of(level)
        return (index + 1) * block + component * HALF + half * segments + segment

    for component in range(2):
        for half in range(halves):
            for tile in range(tiles):
                if tile < halo_tiles:
                    taken, place = left_ref, tile
                elif tile < halo_tiles + own_tiles:
                    taken, place = middle_ref, tile - halo_tiles
                else:
                    taken, place = right_ref, tile - halo_tiles - own_tiles
                turned = taken[component, half, :, place * LANES : (place + 1) * LANES].T
                for inner in range(levels_per_tile):
                    start = start_of(component, half, tile * levels_per_tile + inner)
                    source[pl.ds(start, FB, stride=ROWS), :] = turned[
                        inner * FB : (inner + 1) * FB
                    ]

    def fill_ghosts(buffer):
        for sub in range(FB):
            last = buffer[register(depth, sub), :]
            if mirrored:
                other = jnp.where(
                    segment_row == 0, pltpu.roll(last, ROWS - 1, 0), pltpu.roll(last, 1, 0)
                )
                buffer[register(depth + 1, sub), :] = other
            else:
                buffer[register(0, sub), :] = pltpu.roll(last, 1, 0)
                buffer[register(depth + 1, sub), :] = pltpu.roll(
                    buffer[register(1, sub), :], ROWS - 1, 0
                )

    if mirrored:
        for buffer in (even_buffer, odd_buffer):
            buffer[:block, :] = jnp.zeros((block, LANES), jnp.float32)

    terms = len(weights) - 1

    def begin(index, carry):
        for sub in range(FB):
            here = register(index, sub)
            value = source[here, :]
            swapped[here, :] = side * pltpu.roll(value, HALF, 0)
            even_buffer[here, :] = weights[terms] * value
        return carry

    lax.fori_loop(1, depth + 1, begin, 0)
    fill_ghosts(even_buffer)

    for order in range(terms - 1, -1, -1):
        target, present = (odd_buffer, even_buffer) if order % 2 else (even_buffer, odd_buffer)
        given = swapped if order % 2 else source

        def level_step(index, carry):
            lower = ladder[pl.ds(pl.multiple_of((index - 1) * ROWS, ROWS), ROWS), :]
            upper = ladder[pl.ds(pl.multiple_of(index * ROWS, ROWS), ROWS), :]
            centre = [present[register(index, sub), :] for sub in range(FB)]
            for sub in range(FB):
                here = register(index, sub)
                total = diagonal[register(index - 1, sub), :] * centre[sub]
                total += lower * present[register(index - 1, sub), :]
                total += upper * present[register(index + 1, sub), :]
                if sub > 0:
                    total += sub_ladder[sub] * centre[sub - 1]
                if sub + 1 < FB:
                    total += sub_ladder[sub + 1] * centre[sub + 1]
                if order == 0:
                    total = 0.5 * total
                addend = weights[order] * given[here, :]
                if order < terms - 1:
                    addend -= target[here, :]
                total += addend
                if order == 0:
                    turned = pltpu.roll(total, HALF, 0)
                    total = phase_real * total + phase_imag * (side * turned)
                target[here, :] = total
            return carry

        skipped = (terms - order) // 4 * 4 if mirrored else 0
        lax.fori_loop(1 + skipped, depth + 1, level_step, 0, unroll=4)
        if order > 0:
            fill_ghosts(target)

    matrix = matrix_ref[...]
    for component in range(2):
        for half in range(halves):
            first_column = 0
            for out_ref in out_refs:
                for column in range(0, out_ref.shape[3], LANES):
                    first = (first_column + column) // FB + halo_tiles * levels_per_tile
                    evolved = jnp.concatenate(
                        [
                            even_buffer[
                                pl.ds(start_of(component, half, level), FB, stride=ROWS), :
                            ]
                            for level in range(first, first + levels_per_tile)
                        ],
                        axis=0,
                    )
                    out_ref[component, half, :, column : column + LANES] = lax.dot_general(
                        matrix,
                        evolved,
                        (((1,), (1,)), ((), ())),
                        precision=lax.Precision.HIGHEST,
                        preferred_element_type=jnp.float32,
                    )
                first_column += out_ref.shape[3]


def series_piece(
    scalars, matrix, cutoffs, sides, side_start, middle, first_group, groups, flip, widths
):
    width = middle.shape[3]
    left, right = sides
    halo = left.shape[3]
    halves = 2 if all(number % 2 == 0 for number in (first_group, groups, side_start)) else 1
    segments = HALF // halves
    depth = (width + 2 * halo) // FB // segments
    field = pltpu.VMEM(((depth + 2) * FB * ROWS, LANES), jnp.float32)
    first_unit, first_side = first_group // halves, side_start // halves
    return pl.pallas_call(
        functools.partial(series_kernel, series_weights(DEGREE), halves, flip, first_unit),
        grid=(groups // halves,),
        in_specs=[SCALARS] * len(scalars)
        + [
            pl.BlockSpec((GROUP, GROUP), lambda i: (0, 0)),
            pl.BlockSpec((1, GROUP * halves), lambda i: (0, i + first_unit)),
            pl.BlockSpec((2, halves, GROUP, halo), lambda i: (0, i + first_side, 0, 0)),
            pl.BlockSpec((2, halves, GROUP, width), lambda i: (0, i + first_unit, 0, 0)),
            pl.BlockSpec((2, halves, GROUP, halo), lambda i: (0, i + first_side, 0, 0)),
        ],
        out_specs=[
            pl.BlockSpec((2, halves, GROUP, chunk), lambda i: (0, i, 0, 0)) for chunk in widths
        ],
        out_shape=[
            jax.ShapeDtypeStruct((2, groups, GROUP, chunk), jnp.float32) for chunk in widths
        ],
        scratch_shapes=[
            field,
            field,
            field,
            field,
            pltpu.VMEM(((depth + 1) * ROWS, LANES), jnp.float32),
            pltpu.VMEM((depth * FB * ROWS, LANES), jnp.float32),
        ],
        compiler_params=pltpu.CompilerParams(vmem_limit_bytes=VMEM_LIMIT),
        cost_estimate=pl.CostEstimate(
            flops=groups * SERIES_FLOPS, bytes_accessed=groups * SERIES_BYTES, transcendentals=0
        ),
        name="series",
    )(*scalars, matrix, cutoffs, left, middle, right)


def join_kernel(counts, core_spin, cosines, sines, phase_ref, *refs):
    pieces = len(counts)
    own_refs, other_refs, out_ref = refs[:pieces], refs[pieces : 2 * pieces], refs[-1]
    groups = sum(counts)
    bits = groups.bit_length() - 1
    width = out_ref.shape[3]
    side = (2 * (lax.axis_index("spin") & 1) - 1).astype(jnp.float32)
    core_sine = side * sines[core_spin]
    places = [(piece, index) for piece in range(pieces) for index in range(counts[piece])]

    def row_tile(step, carry):
        rows = pl.ds(pl.multiple_of(step * ROWS, ROWS), ROWS)
        for lanes in range(width // LANES):
            columns = slice(lanes * LANES, (lanes + 1) * LANES)
            fields = []
            for component in range(2):
                field = [
                    cosines[core_spin] * own_refs[piece][component, index, rows, columns]
                    + core_sine * other_refs[piece][component, index, rows, columns]
                    for piece, index in places
                ]
                for bit in range(bits):
                    cosine, sine = cosines[LOW_BITS + bit], sines[LOW_BITS + bit]
                    following = list(field)
                    for group in range(groups):
                        if not (group >> bit) & 1:
                            partner = group | (1 << bit)
                            lower, upper = field[group], field[partner]
                            following[group] = cosine * lower - sine * upper
                            following[partner] = cosine * upper + sine * lower
                    field = following
                fields.append(field)
            for group in range(groups):
                entry = phase_ref[group, rows, :]
                phase_real = jnp.broadcast_to(entry[:, 0:1], (ROWS, LANES))
                phase_imag = jnp.broadcast_to(entry[:, 1:2], (ROWS, LANES))
                real, imag = fields[0][group], fields[1][group]
                out_ref[0, group, rows, columns] = phase_real * real + phase_imag * imag
                out_ref[1, group, rows, columns] = phase_real * imag - phase_imag * real
        return carry

    lax.fori_loop(0, out_ref.shape[2] // ROWS, row_tile, 0)


def join_chunk(core_spin, cosines, sines, table, own, other, target, start, width, out_shape):
    counts = [piece.shape[1] for piece in own]
    groups = sum(counts)
    depth = GROUP // 2
    chunk = start // width

    def spec(piece):
        place = chunk if piece.shape[3] > width else 0
        return pl.BlockSpec((2, piece.shape[1], depth, width), lambda i: (0, 0, i, place))

    operands = [cosines, sines, table, *own, *other]
    in_specs = [
        SCALARS,
        SCALARS,
        pl.BlockSpec((groups, depth, 8), lambda i: (0, i, 0)),
        *[spec(piece) for piece in [*own, *other]],
    ]
    aliases = {}
    if target is not None:
        aliases = {len(operands): 0}
        operands.append(target)
        in_specs.append(pl.BlockSpec(memory_space=pl.ANY))
    return pl.pallas_call(
        functools.partial(join_kernel, counts, core_spin),
        grid=(GROUP // depth,),
        in_specs=in_specs,
        out_specs=pl.BlockSpec((2, groups, depth, width), lambda i: (0, 0, i, chunk)),
        out_shape=jax.ShapeDtypeStruct(out_shape, jnp.float32),
        input_output_aliases=aliases,
        compiler_params=pltpu.CompilerParams(vmem_limit_bytes=VMEM_LIMIT),
        cost_estimate=NO_COST,
        name="join",
    )(*operands)


def partner_term(own_part, partner, cosine, sine_value, phase_bit, side_sign):
    keep_part = 1.0 - phase_bit
    real_part = cosine * own_part[0] + sine_value * (
        side_sign * phase_bit * partner[0] + keep_part * partner[1]
    )
    imag_part = cosine * own_part[1] + sine_value * (
        side_sign * phase_bit * partner[1] - keep_part * partner[0]
    )
    return jnp.stack([real_part, imag_part])


def piece_sizes(groups):
    if groups >= 16:
        unit = groups // 16
        sizes = [4 * unit, unit, unit, 2 * unit, 2 * unit, 2 * unit]
    else:
        sizes = [2, 2]
    return [*sizes, groups - sum(sizes)]


def halo_batches(count):
    if count < 8:
        return [2] + [1] * (count - 2)
    return [2, 1, 2] + [1] * (count - 5)


def chunk_widths(width):
    wide = 2 * LANES
    if width > 2 * wide:
        return [2 * wide] + [wide] * ((width - 3 * wide) // wide) + [LANES, LANES]
    return [wide] * (width // wide - 1) + [LANES, LANES]


def per_device(
    amplitudes,
    cutoffs,
    coupling_first,
    coupling_second,
    frozen_coupling,
    frozen_bits,
    drive_bits,
    angles,
):
    local_configs, width = amplitudes.shape[1:]
    groups = local_configs // GROUP
    local_bits = local_configs.bit_length() - 1
    halo = DEGREE * FB
    spin_count = lax.axis_size("spin")
    fock_count = lax.axis_size("fock")
    spin_place = lax.axis_index("spin")
    core_moves = [(i, i ^ 1) for i in range(spin_count)]
    far_moves = [(i, i ^ 2) for i in range(spin_count)]
    up = [(i, i + 1) for i in range(fock_count - 1)]
    down = [(j, i) for i, j in up]
    core_spin, far_spin = local_bits, local_bits + 1

    field = amplitudes.reshape(2, groups, GROUP, width)
    sizes = piece_sizes(groups)
    starts = [sum(sizes[:index]) for index in range(len(sizes))]
    raw_groups = sizes[0]
    raw = lax.ppermute(field[:, :raw_groups], "spin", far_moves)
    raw_cutoffs = lax.ppermute(cutoffs[: raw_groups * GROUP], "spin", far_moves).reshape(1, -1)
    cutoffs = cutoffs.reshape(1, -1)
    cosines, sines = jnp.cos(angles), jnp.sin(angles)
    matrix, phases = prepare(drive_bits, cosines, sines, local_configs)
    phases = phases.reshape(groups, GROUP, 8)
    others = (coupling_second, frozen_coupling, frozen_bits, drive_bits)

    pieces = [(field, cutoffs, start, size, 0) for start, size in zip(starts, sizes)]
    work = [*pieces, (raw, raw_cutoffs, 0, raw_groups, 2)][1:]
    work.insert(-1, pieces[0])
    last = len(pieces) - 2
    batches = halo_batches(len(work))
    halos = []
    sent = []
    evolved = []
    other = []

    def send_halo(*earlier):
        batch = work[len(halos) : len(halos) + batches[len(sent)]]
        edges = []
        for low, high in ((width - halo, width), (0, halo)):
            source, _, start, _, _ = batch[0]
            count = sum(piece[3] for piece in batch)
            edges.append(source[:, start : start + count, :, low:high])
        if earlier:
            edges = lax.optimization_barrier((*edges, *earlier))[:2]
        sent.append((lax.ppermute(edges[0], "fock", up), lax.ppermute(edges[1], "fock", down)))
        place = 0
        for piece in batch:
            halos.append((sent[-1], place))
            place += piece[3]

    def series(*earlier):
        index = len(evolved)
        source, cuts, start, size, flip = work[index]
        scalars = (tied(coupling_first, *earlier), *others)
        widths = chunk_widths(width) if index == last else [width]
        piece = series_piece(
            scalars, matrix, cuts, *halos[index], source, start, size, flip, widths
        )
        evolved.append(piece)
        if index < last:
            other.append(lax.ppermute(piece[0], "spin", far_moves))
        return piece[0]

    far_sine = jnp.where(spin_place & 2 == 2, sines[far_spin], -sines[far_spin])

    def far_rotated(piece, partner):
        piece = cosines[far_spin] * piece + far_sine * partner
        return piece, lax.ppermute(piece, "spin", core_moves)

    latest = matrix
    landed = {last - 1: [0], last: [1], last + 1: [2], last + 2: [3]}
    send_halo()
    for index in range(len(work)):
        waits = [latest]
        if index == min(3, last):
            waits.append(raw)
        waits += [other[place] for place in landed.get(index, []) if place < len(other)]
        if index == 0 and len(sent) < len(batches):
            send_halo(*sent[0])
        latest = series(*waits)
        if index not in (1, 2) and len(sent) < len(batches):
            send_halo(latest)
    pairs = [far_rotated(evolved[last + 1][0], evolved[last + 2][0])]
    pairs += [far_rotated(piece[0], partner) for piece, partner in zip(evolved, other)]
    received = [lax.ppermute(piece, "spin", far_moves) for piece in evolved[last][:2]]
    result = None
    start = 0
    for chunk, piece in enumerate(evolved[last]):
        chunk_pairs = [*pairs, far_rotated(piece, received[chunk])]
        result = join_chunk(
            core_spin,
            cosines,
            sines,
            phases,
            [pair[0] for pair in chunk_pairs],
            [pair[1] for pair in chunk_pairs],
            result,
            start,
            piece.shape[3],
            field.shape,
        )
        start += piece.shape[3]
        if chunk + 2 < len(evolved[last]):
            going, result = lax.optimization_barrier((evolved[last][chunk + 2], result))
            received.append(lax.ppermute(going, "spin", far_moves))
    result = result.reshape(amplitudes.shape)
    for bit in range(2, spin_count.bit_length() - 1):
        spin = local_bits + bit
        partner = lax.ppermute(result, "spin", [(i, i ^ (1 << bit)) for i in range(spin_count)])
        side = jnp.where((spin_place >> bit) & 1 == 1, 1.0, -1.0)
        result = partner_term(
            result, partner, cosines[spin], sines[spin], drive_bits[spin].astype(jnp.float32), side
        )
    return result


def solution(mesh):
    placed = (P(None, "spin", "fock"), P("spin"), P(), P(), P(), P(), P(), P())
    return jax.shard_map(
        per_device, mesh=mesh, in_specs=placed, out_specs=P(None, "spin", "fock"), check_vma=False
    )
```
